32 devices in a mesh: groups: 2 (over x), dom: 8 (over z, y), shard: 2 (over core).
Axes of the slice: x: 2, y: 2, z: 4, core: 2. Of those that a mesh axis runs over, the one named last changes fastest.
Arguments:
- entity_table: float32 [8192, 400], P(('groups', 'dom'), 'shard'), parts along dimension 0, may hold values from -1.8 to 1.8
- relation_table: float32 [128, 400], P('groups'), parts along dimension 0, may hold values from -4.8 to 4.8
- round_shift: int32 [1], replicated, may hold values from 1 to 7
- head_rows: int32 [64, 1024], P(('groups', 'dom', 'shard')), parts along dimension 0, may hold values from 0 to 511
- tail_rows: int32 [64, 1024], P(('groups', 'dom', 'shard')), parts along dimension 0, may hold values from 0 to 511
- relation_ids: int32 [64, 1024], P(('groups', 'dom', 'shard')), parts along dimension 0, may hold values from 0 to 63
- negative_rows: int32 [64, 1024], P(('groups', 'dom', 'shard')), parts along dimension 0, may hold values from 0 to 511
- live_edges: int32 [64], P(('groups', 'dom', 'shard')), parts along dimension 0, may hold values from 256 to 1024
Outputs:
- entity_grad: float32 [8192, 400], P(('groups', 'dom'), 'shard'), parts along dimension 0
The draws below stay inside these ranges and needn't reach their ends.
There are 2 independent parts, one for each index of `groups`. The reference program is written for one: setup_inputs(seed, part) draws one part's arguments, and reference() takes and returns one part's arrays. A program takes and returns all parts, laid end to end along the dimension named above; an argument that names none is the same for every part. Nothing has to cross between parts.
Inputs may be any that keep to these rules, and one draw needn't show every extreme that they name: Partition p is paired with partition (p + round_shift) mod 8; the same plan serves every group.
All inputs are finite; a program needn't handle non-finite values.
Results may differ from the reference program's by a relative error of at most 0.0047.
Values may be sent and summed in bfloat16 or wider, within the bound.
A program may use at most 64 MiB of HBM per device.

```python
import math
import jax
import jax.numpy as jnp
import numpy as np
from jax import lax

D = 400
NREL = 64
ROWS = 512
EDGES = 1024
NEG = 1024
PARTITIONS = 8
ENT = 4096
SLOTS = 32
N_DOM = 8
N_SHARD = 2


def with_ends(result, rng, least, top_value):
    longest = result.shape.index(max(result.shape))
    spots = []
    for shift in (0, 1):
        where = [jax.random.randint(jax.random.fold_in(rng, axis), (), 0, length) for axis, length in enumerate(result.shape)]
        where[longest] = (where[longest] + shift) % result.shape[longest]
        spots.append(tuple(where))
    return result.at[spots[0]].set(least).at[spots[1]].set(top_value)


def levels(stream_key, dims, shards, smallest, top_value):
    gain, own = 1.0, jax.random.fold_in(stream_key, 6)
    for dim, blocks in shards:
        heights = jnp.exp(jax.random.uniform(jax.random.fold_in(own, dim), (blocks,), jnp.float32, smallest / len(shards), top_value / len(shards)))
        gain = gain * jnp.repeat(heights, dims[dim] // blocks).reshape([-1 if axis == dim else 1 for axis in range(len(dims))])
    return gain


def rank_table(count, slope):
    loads = [(1 << 20) // math.isqrt(rank ** slope) + 1 for rank in range(1, count + 1)]
    spread = 1 + sum(loads) // (1 << 30)
    return np.cumsum(np.array([max(1, weight // spread) for weight in loads]))


def skewed_ids(rng, extent, amount, lean):
    grid = rank_table(amount, lean)
    pick = jax.random.randint(jax.random.fold_in(rng, 1), extent, 0, int(grid[amount - 1]))
    rank = jnp.searchsorted(jnp.asarray(grid, jnp.int32), pick, side="right")
    return jax.random.permutation(jax.random.fold_in(rng, 2), amount)[rank].astype(jnp.int32)


def normal_values(stream_key, dims, width, reach, shards=(), kind=jnp.bfloat16):
    array = jax.random.normal(stream_key, dims, jnp.float32) * width
    if len(shards) > 0:
        array = levels(stream_key, dims, shards, -0.22, 0.18) * array
    return jnp.clip(array, min=-reach, max=reach).astype(kind)


def setup_inputs(seed: int = 0, part: int = 0) -> dict:
    key_of = jax.random.split(jax.random.key(seed), 9)
    part_keys = jax.random.split(jax.random.fold_in(key_of[8], part), 9)
    entity_table = normal_values(part_keys[0], (ENT, D), 0.3, 1.8, ((0, 8), (1, 2)), jnp.float32)
    relation_table = normal_values(part_keys[1], (NREL, D), 0.8, 4.8, (), jnp.float32)
    round_shift = jax.random.randint(key_of[2], (1,), 1, PARTITIONS).astype(jnp.int32)
    head_rows = with_ends(jax.random.randint(part_keys[3], (SLOTS, EDGES), 0, ROWS), jax.random.fold_in(part_keys[3], 1), 0, ROWS - 1).astype(jnp.int32)
    tail_rows = with_ends(jax.random.randint(part_keys[4], (SLOTS, EDGES), 0, ROWS), jax.random.fold_in(part_keys[4], 1), 0, ROWS - 1).astype(jnp.int32)
    relation_ids = with_ends(skewed_ids(part_keys[5], (SLOTS, EDGES), NREL, 2), jax.random.fold_in(part_keys[5], 3), 0, NREL - 1).astype(jnp.int32)
    negative_rows = with_ends(jax.random.randint(part_keys[6], (SLOTS, NEG), 0, ROWS), jax.random.fold_in(part_keys[6], 1), 0, ROWS - 1).astype(jnp.int32)
    live_edges = with_ends(jax.random.randint(part_keys[7], (SLOTS,), EDGES // 4, EDGES + 1), jax.random.fold_in(part_keys[7], 1), EDGES // 4, EDGES).astype(jnp.int32)
    return {"entity_table": entity_table, "relation_table": relation_table, "round_shift": round_shift, "head_rows": head_rows, "tail_rows": tail_rows, "relation_ids": relation_ids, "negative_rows": negative_rows, "live_edges": live_edges}


def complex_product(left_rows, right_rows):
    row_shape = left_rows.shape
    split_shape = row_shape[:-1] + (N_SHARD, 2, D // (2 * N_SHARD))
    left_parts = left_rows.reshape(split_shape)
    right_parts = right_rows.reshape(split_shape)
    real_part = left_parts[..., 0, :] * right_parts[..., 0, :] - left_parts[..., 1, :] * right_parts[..., 1, :]
    imag_part = left_parts[..., 0, :] * right_parts[..., 1, :] + left_parts[..., 1, :] * right_parts[..., 0, :]
    return jnp.stack([real_part, imag_part], axis=-2).reshape(row_shape)


def conjugate_product(grad_rows, right_rows):
    row_shape = grad_rows.shape
    split_shape = row_shape[:-1] + (N_SHARD, 2, D // (2 * N_SHARD))
    grad_parts = grad_rows.reshape(split_shape)
    right_parts = right_rows.reshape(split_shape)
    real_part = grad_parts[..., 0, :] * right_parts[..., 0, :] + grad_parts[..., 1, :] * right_parts[..., 1, :]
    imag_part = grad_parts[..., 1, :] * right_parts[..., 0, :] - grad_parts[..., 0, :] * right_parts[..., 1, :]
    return jnp.stack([real_part, imag_part], axis=-2).reshape(row_shape)


def reference(entity_table, relation_table, round_shift, head_rows, tail_rows, relation_ids, negative_rows, live_edges):
    low_table = entity_table.astype(jnp.bfloat16).reshape(N_DOM, ROWS, D)
    per_part = SLOTS // N_DOM
    head_all = head_rows.reshape(N_DOM, per_part, EDGES)
    tail_all = tail_rows.reshape(N_DOM, per_part, EDGES)
    relation_all = relation_ids.reshape(N_DOM, per_part, EDGES)
    negative_all = negative_rows.reshape(N_DOM, per_part, NEG)
    live_all = live_edges.reshape(N_DOM, per_part)
    offset = round_shift[0]
    neg_scale = NEG ** -0.5

    def one_partition(part_index):
        own_block = low_table[part_index]
        partner_block = low_table[(part_index + offset) % N_DOM]
        own_grad = jnp.zeros((ROWS, D), jnp.float32)
        partner_grad = jnp.zeros((ROWS, D), jnp.float32)
        for slot_index in range(per_part):
            head_index = head_all[part_index, slot_index]
            tail_index = tail_all[part_index, slot_index]
            negative_index = negative_all[part_index, slot_index]
            relation_rows = relation_table[relation_all[part_index, slot_index]]
            queries = complex_product(own_block[head_index].astype(jnp.float32), relation_rows).astype(jnp.bfloat16)
            tail_vectors = partner_block[tail_index]
            negative_vectors = partner_block[negative_index]
            live_mask = (jnp.arange(EDGES) < live_all[part_index, slot_index]).astype(jnp.float32)
            positive = jnp.sum(queries.astype(jnp.float32) * tail_vectors.astype(jnp.float32), axis=1)
            negative = jnp.dot(queries, negative_vectors.T, preferred_element_type=jnp.float32)
            tail_coef = -live_mask * jax.nn.sigmoid(-positive)
            neg_coef = (live_mask[:, None] * jax.nn.sigmoid(negative) * neg_scale).astype(jnp.bfloat16)
            grad_query = (tail_coef[:, None] * tail_vectors.astype(jnp.float32)
                          + jnp.dot(neg_coef, negative_vectors, preferred_element_type=jnp.float32)).astype(jnp.bfloat16)
            own_grad = own_grad.at[head_index].add(conjugate_product(grad_query.astype(jnp.float32), relation_rows))
            partner_grad = partner_grad.at[tail_index].add(tail_coef[:, None] * queries.astype(jnp.float32))
            partner_grad = partner_grad.at[negative_index].add(jnp.dot(neg_coef.T, queries, preferred_element_type=jnp.float32))
        return own_grad, partner_grad

    own_grads, partner_grads = lax.map(one_partition, jnp.arange(N_DOM, dtype=jnp.int32))
    rounded = lax.optimization_barrier(partner_grads.astype(jnp.bfloat16))
    source_index = ((jnp.arange(N_DOM, dtype=jnp.int32) - offset) % N_DOM).astype(jnp.int32)
    shifted = rounded[source_index]
    combined = own_grads + shifted.astype(jnp.float32)
    return combined.reshape(ENT, D)
```

```python
import functools

import jax
import jax.numpy as jnp
from jax import lax
from jax.experimental import pallas as pl
from jax.experimental.pallas import tpu as pltpu
from jax.sharding import PartitionSpec as P

MESH = pl.DeviceIdType.MESH
BF16 = jnp.bfloat16
F32 = jnp.float32
NN = (((1,), (0,)), ((), ()))
NT = (((1,), (1,)), ((), ()))
TN = (((0,), (0,)), ((), ()))
CHUNKS = 2


def mm(left, right, dims):
    return lax.dot_general(left, right, dims, preferred_element_type=F32)


def padded(parts):
    return -(-parts // 8) * 8


def select_columns(parts, width, first):
    pad = padded(parts)
    row = lax.broadcasted_iota(jnp.int32, (2 * pad, width), 0)
    col = lax.broadcasted_iota(jnp.int32, (2 * pad, width), 1) - first
    real = (row < parts) & (col == row)
    imag = (row >= pad) & (row < pad + parts) & (col == row - pad + parts)
    return jnp.where(real | imag, 1.0, 0.0).astype(BF16)


def one_hot(ids, count, first=0, modulus=None):
    row = lax.broadcasted_iota(jnp.int32, (count, ids.shape[1]), 0)
    if modulus is not None:
        row = jnp.where(row >= modulus, row - modulus, row)
    return row + first == ids


def kernel(
    shift, n_dom, table, rel, head, tail, rid, neg, live, out,
    own, part, query, rel_edge, hot, count, grad_query, pair_send, pair_recv, home_send, home_recv,
    own_send, own_recv, send_sem, recv_sem,
):
    rows, half_width = table.shape
    parts = half_width // 2
    pad = padded(parts)
    half = 2 * pad
    blocks, edges = head.shape
    relations = rel.shape[0]
    chunk = rows // CHUNKS
    scale = 0.5 * neg.shape[1] ** (-0.5)
    side = lax.axis_index("shard")
    me = lax.axis_index("dom")
    mate = {"shard": 1 - side}
    asker = {"dom": lax.rem(me + n_dom - shift, n_dom)}
    partner = {"dom": lax.rem(me + shift, n_dom)}

    def copy(index, source, target, device):
        return pltpu.make_async_remote_copy(
            src_ref=source, dst_ref=target, send_sem=send_sem.at[index],
            recv_sem=recv_sem.at[index], device_id=device, device_id_type=MESH,
        )

    barrier = pltpu.get_barrier_semaphore()
    for device in (mate, asker, partner):
        pl.semaphore_signal(barrier, inc=1, device_id=device, device_id_type=MESH)
    choose = select_columns(parts, half_width, 0)
    own[0:half] = mm(choose, table[...].astype(BF16), NT).astype(BF16)
    pl.semaphore_wait(barrier, 3)

    own_copy = copy(0, own.at[pl.ds(0, half)], own.at[pl.ds(half, half)], mate)
    own_copy.start()
    table_copies = []
    for c in range(CHUNKS):
        table_copies.append(
            copy(1 + c, own.at[pl.ds(0, half), pl.ds(c * chunk, chunk)], part.at[c, pl.ds(0, half)], asker)
        )
        table_copies[c].start()
    forward_copies = [
        copy(1 + CHUNKS + c, part.at[c, pl.ds(0, half)], part.at[c, pl.ds(half, half)], mate)
        for c in range(CHUNKS)
    ]
    pair_copies = [
        copy(1 + 2 * CHUNKS + c, pair_send.at[c], pair_recv.at[c], mate) for c in range(CHUNKS)
    ]
    home_copies = [
        copy(1 + 3 * CHUNKS + c, home_send.at[c], home_recv.at[c], partner) for c in range(CHUNKS)
    ]
    grad_copy = copy(1 + 4 * CHUNKS, own_send, own_recv, mate)

    wide = rel[...]
    high = wide.astype(BF16)
    low = (wide - high.astype(F32)).astype(BF16)
    pieces = jnp.concatenate([high, low], axis=0)
    choose_all = jnp.concatenate(
        [
            select_columns(parts, 2 * half_width, side * half_width),
            select_columns(parts, 2 * half_width, (1 - side) * half_width),
        ],
        axis=0,
    )
    rel_rows = mm(choose_all, pieces, NT).astype(BF16)
    edge_index = lax.broadcasted_iota(jnp.int32, (1, edges), 1)
    for b in range(blocks):
        pick = jnp.where(one_hot(rid[b : b + 1], 2 * relations, 0, relations), 1.0, 0.0).astype(BF16)
        rel_edge[b] = mm(rel_rows, pick, NN)
        live_head = jnp.where(edge_index < live[b], head[b : b + 1], -1)
        hot[b] = jnp.where(one_hot(live_head, rows), 1.0, 0.0).astype(BF16)
        seen = jnp.where(one_hot(neg[b : b + 1], rows), scale, 0.0)
        count[b] = jnp.sum(seen, axis=1, keepdims=True)

    own_copy.wait_recv()
    for b in range(blocks):
        heads = mm(own[...], hot[b], NN)
        for j in range(2):
            real, imag = j * half, j * half + pad
            h_re, h_im = heads[real:imag], heads[imag : imag + pad]
            r_re, r_im = rel_edge[b, real:imag], rel_edge[b, imag : imag + pad]
            query[b, real : real + half] = jnp.concatenate(
                [h_re * r_re - h_im * r_im, h_re * r_im + h_im * r_re], axis=0
            ).astype(BF16)
        if b < CHUNKS:
            table_copies[b].wait_recv()
            forward_copies[b].start()
    for c in range(blocks, CHUNKS):
        table_copies[c].wait_recv()
        forward_copies[c].start()

    def send_home(c, kept):
        pair_copies[c].wait_recv()
        home_send[c] = (kept + pair_recv[c].astype(F32)).astype(BF16)
        home_copies[c].start()

    kept = None
    for c in range(CHUNKS):
        forward_copies[c].wait_recv()
        partner_rows = part[c]
        total = jnp.zeros((2 * half, chunk), F32)
        for b in range(blocks):
            score = mm(partner_rows, query[b], TN)
            curve = jnp.tanh(0.5 * score)
            at_tail = jnp.where(one_hot(tail[b : b + 1], chunk, c * chunk), 0.5, 0.0)
            weight = count[b, c * chunk : (c + 1) * chunk]
            coef = ((weight - at_tail) + curve * (weight + at_tail)).astype(BF16)
            step = mm(partner_rows, coef, NN)
            grad_query[b] = step if c == 0 else grad_query[b] + step
            total = total + mm(query[b], coef, NT)
        pair_send[c] = total[half:].astype(BF16)
        pair_copies[c].start()
        if c > 0:
            send_home(c - 1, kept)
        kept = total[0:half]

    own_total = jnp.zeros((2 * half, rows), F32)
    for b in range(blocks):
        halves = []
        for j in range(2):
            real, imag = j * half, j * half + pad
            grads = grad_query[b, real : real + half].astype(BF16).astype(F32)
            g_re, g_im = grads[0:pad], grads[pad:half]
            r_re, r_im = rel_edge[b, real:imag], rel_edge[b, imag : imag + pad]
            halves += [g_re * r_re + g_im * r_im, g_im * r_re - g_re * r_im]
        own_total = own_total + mm(jnp.concatenate(halves, axis=0).astype(BF16), hot[b], NT)
        if b == 0:
            send_home(CHUNKS - 1, kept)
    own_send[...] = own_total[half:].astype(BF16)
    grad_copy.start()
    own_high = own_total[0:half].astype(BF16)
    own_low = (own_total[0:half] - own_high.astype(F32)).astype(BF16)
    choose_two = jnp.concatenate([choose, choose], axis=0)
    out[...] = mm(jnp.concatenate([own_high, own_low], axis=0), choose_two, TN)
    grad_copy.wait_recv()
    for c in range(CHUNKS):
        home_copies[c].wait_recv()
        span = slice(c * chunk, (c + 1) * chunk)
        arrived = jnp.concatenate([own_recv[:, span], home_recv[c]], axis=0)
        out[span] = out[span] + mm(arrived, choose_two, TN)
    for done in [own_copy, grad_copy] + table_copies + forward_copies + pair_copies + home_copies:
        done.wait_send()


def fused(shift, n_dom, table, rel, head, tail, rid, neg, live):
    rows, half_width = table.shape
    blocks, edges = head.shape
    half = 2 * padded(half_width // 2)
    chunk = rows // CHUNKS
    copies = 2 + 4 * CHUNKS
    vmem = pl.BlockSpec(memory_space=pltpu.VMEM)
    return pl.pallas_call(
        functools.partial(kernel, shift, n_dom),
        out_shape=jax.ShapeDtypeStruct((rows, half_width), F32),
        in_specs=[vmem] * 6 + [pl.BlockSpec(memory_space=pltpu.SMEM)],
        out_specs=vmem,
        scratch_shapes=[
            pltpu.VMEM((2 * half, rows), BF16),
            pltpu.VMEM((CHUNKS, 2 * half, chunk), BF16),
            pltpu.VMEM((blocks, 2 * half, edges), BF16),
            pltpu.VMEM((blocks, 2 * half, edges), F32),
            pltpu.VMEM((blocks, rows, edges), BF16),
            pltpu.VMEM((blocks, rows, 1), F32),
            pltpu.VMEM((blocks, 2 * half, edges), F32),
            pltpu.VMEM((CHUNKS, half, chunk), BF16),
            pltpu.VMEM((CHUNKS, half, chunk), BF16),
            pltpu.VMEM((CHUNKS, half, chunk), BF16),
            pltpu.VMEM((CHUNKS, half, chunk), BF16),
            pltpu.VMEM((half, rows), BF16),
            pltpu.VMEM((half, rows), BF16),
            pltpu.SemaphoreType.DMA((copies,)),
            pltpu.SemaphoreType.DMA((copies,)),
        ],
        compiler_params=pltpu.CompilerParams(
            collective_id=shift - 1, has_side_effects=True, vmem_limit_bytes=48 * 1024 * 1024
        ),
    )(table, rel, head, tail, rid, neg, live)


def local(table, rel, round_shift, head, tail, rid, neg, live):
    n_dom = lax.axis_size("dom")
    branches = [functools.partial(fused, shift, n_dom) for shift in range(1, n_dom)]
    return lax.switch(round_shift[0] - 1, branches, table, rel, head, tail, rid, neg, live)


def shifted(value, axis, steps):
    count = lax.axis_size(axis)
    pairs = [(source, (source + steps) % count) for source in range(count)]
    return lax.ppermute(value, axis, pairs)


def complex_product(left_rows, right_rows, halves):
    row_shape = left_rows.shape
    split_shape = row_shape[:-1] + (halves, 2, row_shape[-1] // (2 * halves))
    left_parts = left_rows.reshape(split_shape)
    right_parts = right_rows.reshape(split_shape)
    real_part = (
        left_parts[..., 0, :] * right_parts[..., 0, :]
        - left_parts[..., 1, :] * right_parts[..., 1, :]
    )
    imag_part = (
        left_parts[..., 0, :] * right_parts[..., 1, :]
        + left_parts[..., 1, :] * right_parts[..., 0, :]
    )
    return jnp.stack([real_part, imag_part], axis=-2).reshape(row_shape)


def conjugate_product(grad_rows, right_rows, halves):
    row_shape = grad_rows.shape
    split_shape = row_shape[:-1] + (halves, 2, row_shape[-1] // (2 * halves))
    grad_parts = grad_rows.reshape(split_shape)
    right_parts = right_rows.reshape(split_shape)
    real_part = (
        grad_parts[..., 0, :] * right_parts[..., 0, :]
        + grad_parts[..., 1, :] * right_parts[..., 1, :]
    )
    imag_part = (
        grad_parts[..., 1, :] * right_parts[..., 0, :]
        - grad_parts[..., 0, :] * right_parts[..., 1, :]
    )
    return jnp.stack([real_part, imag_part], axis=-2).reshape(row_shape)


def pick_relations(ids, table):
    relation_index = jnp.arange(table.shape[0], dtype=jnp.int32)
    selector = (ids[:, None] == relation_index[None, :]).astype(jnp.float32)
    return jnp.dot(selector, table, precision=lax.Precision.HIGHEST)


def score_block(queries, tail_vectors, negative_vectors, live_count, neg_scale):
    edge_count = queries.shape[0]
    live_mask = (jnp.arange(edge_count, dtype=jnp.int32) < live_count).astype(jnp.float32)
    query_wide = queries.astype(jnp.float32)
    positive = jnp.sum(query_wide * tail_vectors.astype(jnp.float32), axis=1)
    negative = lax.dot_general(
        queries, negative_vectors, (((1,), (1,)), ((), ())), preferred_element_type=jnp.float32
    )
    tail_coef = -live_mask * jax.nn.sigmoid(-positive)
    neg_coef = (live_mask[:, None] * jax.nn.sigmoid(negative) * neg_scale).astype(jnp.bfloat16)
    grad_query = (
        tail_coef[:, None] * tail_vectors.astype(jnp.float32)
        + jnp.dot(neg_coef, negative_vectors, preferred_element_type=jnp.float32)
    ).astype(jnp.bfloat16)
    neg_grad = lax.dot_general(
        neg_coef, queries, (((0,), (0,)), ((), ())), preferred_element_type=jnp.float32
    )
    return (grad_query, tail_coef[:, None] * query_wide, neg_grad)


def local_hops(
    entity_table,
    relation_table,
    round_shift,
    head_rows,
    tail_rows,
    relation_ids,
    negative_rows,
    live_edges,
):
    row_count = entity_table.shape[0]
    full_width = relation_table.shape[1]
    halves = lax.axis_size("shard")
    block_count = head_rows.shape[0]
    neg_scale = negative_rows.shape[1] ** (-0.5)
    hop_count = (lax.axis_size("dom") - 1).bit_length()
    offset = round_shift[0]
    own_low = entity_table.astype(jnp.bfloat16)
    own_table = lax.all_gather(own_low, "shard", axis=1, tiled=True)
    relation_list = [
        pick_relations(relation_ids[block_index], relation_table)
        for block_index in range(block_count)
    ]
    partner_grad = jnp.zeros((row_count, full_width), jnp.float32)
    partner_half = own_low
    for bit_index in range(hop_count):
        arrived = shifted(partner_half, "dom", -(1 << bit_index))
        take_hop = offset // (1 << bit_index) % 2 == 1
        partner_half = jnp.where(take_hop, arrived, partner_half)
    partner_table = lax.all_gather(partner_half, "shard", axis=1, tiled=True)
    grad_list = []
    for block_index in range(block_count):
        head_vectors = own_table[head_rows[block_index]].astype(jnp.float32)
        queries = complex_product(head_vectors, relation_list[block_index], halves).astype(
            jnp.bfloat16
        )
        grad_query, tail_grad, neg_grad = score_block(
            queries,
            partner_table[tail_rows[block_index]],
            partner_table[negative_rows[block_index]],
            live_edges[block_index],
            neg_scale,
        )
        partner_grad = partner_grad.at[tail_rows[block_index]].add(tail_grad)
        partner_grad = partner_grad.at[negative_rows[block_index]].add(neg_grad)
        grad_list.append(grad_query)
    returned = jnp.stack(grad_list)
    own_grad = jnp.zeros((row_count, full_width), jnp.float32)
    for block_index in range(block_count):
        own_grad = own_grad.at[head_rows[block_index]].add(
            conjugate_product(
                returned[block_index].astype(jnp.float32), relation_list[block_index], halves
            )
        )
    partner_sum, own_sum = (
        lax.psum_scatter(partner_grad, "shard", scatter_dimension=1, tiled=True),
        lax.psum_scatter(own_grad, "shard", scatter_dimension=1, tiled=True),
    )
    going_back = partner_sum.astype(jnp.bfloat16)
    for bit_index in range(hop_count):
        arrived = shifted(going_back, "dom", 1 << bit_index)
        take_hop = offset // (1 << bit_index) % 2 == 1
        going_back = jnp.where(take_hop, arrived, going_back)
    return own_sum + going_back.astype(jnp.float32)


def solution(mesh):
    in_specs = (
        P(("groups", "dom"), "shard"),
        P("groups", None),
        P(),
        P(("groups", "dom", "shard"), None),
        P(("groups", "dom", "shard"), None),
        P(("groups", "dom", "shard"), None),
        P(("groups", "dom", "shard"), None),
        P(("groups", "dom", "shard")),
    )
    out_specs = P(("groups", "dom"), "shard")
    return jax.shard_map(
        local if mesh.shape["dom"] <= 8 else local_hops,
        mesh=mesh, in_specs=in_specs, out_specs=out_specs, check_vma=False)
```

```python
import functools

import jax
import jax.numpy as jnp
from jax import lax
from jax.experimental import pallas as pl
from jax.experimental.pallas import tpu as pltpu
from jax.sharding import PartitionSpec as P

MESH = pl.DeviceIdType.MESH
BF16 = jnp.bfloat16
F32 = jnp.float32
NN = (((1,), (0,)), ((), ()))
NT = (((1,), (1,)), ((), ()))
TN = (((0,), (0,)), ((), ()))
CHUNKS = 2
TILE = 512


def mm(left, right, dims):
    return lax.dot_general(left, right, dims, preferred_element_type=F32)


def padded(parts):
    return -(-parts // 8) * 8


def select_columns(parts, width, first):
    pad = padded(parts)
    row = lax.broadcasted_iota(jnp.int32, (2 * pad, width), 0)
    col = lax.broadcasted_iota(jnp.int32, (2 * pad, width), 1) - first
    real = (row < parts) & (col == row)
    imag = (row >= pad) & (row < pad + parts) & (col == row - pad + parts)
    return jnp.where(real | imag, 1.0, 0.0).astype(BF16)


def one_hot(ids, count, first=0, modulus=None):
    row = lax.broadcasted_iota(jnp.int32, (count, ids.shape[1]), 0)
    if modulus is not None:
        row = jnp.where(row >= modulus, row - modulus, row)
    return row + first == ids


def kernel(
    shift, n_dom, table, rel, head, tail, rid, neg, live, out,
    own, part, part_rows, query, rel_edge, hot, count, grad_query, total, own_total,
    pair_send, pair_recv, home_send, home_recv, own_send, own_recv, send_sem, recv_sem,
):
    half_width, rows = table.shape
    parts = half_width // 2
    pad = padded(parts)
    half = 2 * pad
    blocks, edges = head.shape
    relations = rel.shape[0]
    chunk = rows // CHUNKS
    tiles = edges // TILE
    scale = 0.5 * neg.shape[1] ** (-0.5)
    side = lax.axis_index("shard")
    me = lax.axis_index("dom")
    mate = {"shard": 1 - side}
    asker = {"dom": lax.rem(me + n_dom - shift, n_dom)}
    partner = {"dom": lax.rem(me + shift, n_dom)}

    def copy(index, source, target, device):
        return pltpu.make_async_remote_copy(
            src_ref=source, dst_ref=target, send_sem=send_sem.at[index],
            recv_sem=recv_sem.at[index], device_id=device, device_id_type=MESH,
        )

    barrier = pltpu.get_barrier_semaphore()
    for device in (mate, asker, partner):
        pl.semaphore_signal(barrier, inc=1, device_id=device, device_id_type=MESH)
    choose = select_columns(parts, half_width, 0)
    mine = mm(choose, table[...].astype(BF16), NN).astype(BF16)
    for c in range(CHUNKS):
        own[c, 0:half] = mine[:, c * chunk : (c + 1) * chunk]
    pl.semaphore_wait(barrier, 3)

    low_half, high_half = pl.ds(0, half), pl.ds(half, half)

    def own_copy(c):
        return copy(c, own.at[c, low_half], own.at[c, high_half], mate)

    def table_copy(c):
        return copy(CHUNKS + c, own.at[c, low_half], part.at[c, low_half], asker)

    def forward_copy(c):
        return copy(2 * CHUNKS + c, part.at[c, low_half], part.at[c, high_half], mate)

    def pair_copy(c):
        return copy(3 * CHUNKS + c, pair_send.at[c], pair_recv.at[c], mate)

    def home_copy(c):
        return copy(4 * CHUNKS + c, home_send.at[c], home_recv.at[c], partner)

    grad_copy = copy(5 * CHUNKS, own_send, own_recv, mate)
    for c in range(CHUNKS):
        own_copy(c).start()
        table_copy(c).start()

    wide = rel[...]
    high = wide.astype(BF16)
    low = (wide - high.astype(F32)).astype(BF16)
    pieces = jnp.concatenate([high, low], axis=0)
    choose_all = jnp.concatenate(
        [
            select_columns(parts, 2 * half_width, side * half_width),
            select_columns(parts, 2 * half_width, (1 - side) * half_width),
        ],
        axis=0,
    )
    rel_rows = mm(choose_all, pieces, NT).astype(BF16)
    count[...] = jnp.zeros_like(count)

    def place(t):
        b = t // tiles
        first = pl.multiple_of((t - b * tiles) * TILE, TILE)
        return b, first

    def index_step(t, _):
        b, first = place(t)
        spot = (pl.ds(b, 1), pl.ds(first, TILE))
        pick = jnp.where(one_hot(rid[spot], 2 * relations, 0, relations), 1.0, 0.0).astype(BF16)
        rel_edge[t] = mm(rel_rows, pick, NN)
        edge_index = first + lax.broadcasted_iota(jnp.int32, (1, TILE), 1)
        live_head = jnp.where(edge_index < live[b], head[spot], -1)
        hot[t] = jnp.where(one_hot(live_head, rows), 1.0, 0.0).astype(BF16)
        seen = jnp.where(one_hot(neg[spot], rows), scale, 0.0)
        count[b] = count[b] + jnp.sum(seen, axis=1, keepdims=True)
        return 0

    lax.fori_loop(0, blocks * tiles, index_step, 0)
    for c in range(CHUNKS):
        own_copy(c).wait_recv()

    def query_step(t, _):
        heads = sum(mm(own[c], hot[t, c * chunk : (c + 1) * chunk], NN) for c in range(CHUNKS))
        for j in range(2):
            real, imag = j * half, j * half + pad
            h_re, h_im = heads[real:imag], heads[imag : imag + pad]
            r_re, r_im = rel_edge[t, real:imag], rel_edge[t, imag : imag + pad]
            query[t, real : real + half] = jnp.concatenate(
                [h_re * r_re - h_im * r_im, h_re * r_im + h_im * r_re], axis=0
            ).astype(BF16)
        grad_query[t] = jnp.zeros_like(grad_query[t])
        return 0

    lax.fori_loop(0, blocks * tiles, query_step, 0)
    for c in range(CHUNKS):
        table_copy(c).wait_recv()
        forward_copy(c).start()

    def send_home(c):
        pair_copy(c).wait_recv()
        home_send[c] = (total[c, 0:half] + pair_recv[c].astype(F32)).astype(BF16)
        home_copy(c).start()

    row_index = lax.broadcasted_iota(jnp.int32, (chunk, chunk), 0)
    col_index = lax.broadcasted_iota(jnp.int32, (chunk, chunk), 1)
    same = jnp.where(row_index == col_index, 1.0, 0.0).astype(BF16)

    def chunk_step(c, _):
        forward_copy(c).wait_recv()
        part_rows[...] = mm(same, part[c], NT).astype(BF16)
        total[c] = jnp.zeros_like(total[c])
        start = pl.multiple_of(c * chunk, chunk)

        def score_step(t, _):
            b, first = place(t)
            score = mm(part_rows[...], query[t], NN)
            curve = jnp.tanh(0.5 * score)
            ids = tail[pl.ds(b, 1), pl.ds(first, TILE)]
            at_tail = jnp.where(one_hot(ids, chunk, start), 0.5, 0.0)
            weight = count[b, pl.ds(start, chunk)]
            coef = ((weight - at_tail) + curve * (weight + at_tail)).astype(BF16)
            grad_query[t] = grad_query[t] + mm(part[c], coef, NN)
            total[c] = total[c] + mm(query[t], coef, NT)
            return 0

        lax.fori_loop(0, blocks * tiles, score_step, 0)
        pair_send[c] = total[c, half : 2 * half].astype(BF16)
        pair_copy(c).start()

        @pl.when(c > 0)
        def _():
            send_home(c - 1)

        return 0

    lax.fori_loop(0, CHUNKS, chunk_step, 0)
    own_total[...] = jnp.zeros_like(own_total)

    def own_step(t, _):
        halves = []
        for j in range(2):
            real, imag = j * half, j * half + pad
            grads = grad_query[t, real : real + half].astype(BF16).astype(F32)
            g_re, g_im = grads[0:pad], grads[pad:half]
            r_re, r_im = rel_edge[t, real:imag], rel_edge[t, imag : imag + pad]
            halves += [g_re * r_re + g_im * r_im, g_im * r_re - g_re * r_im]
        own_total[...] = own_total[...] + mm(jnp.concatenate(halves, axis=0).astype(BF16), hot[t], NT)

        @pl.when(t == 0)
        def _():
            send_home(CHUNKS - 1)

        return 0

    lax.fori_loop(0, blocks * tiles, own_step, 0)
    own_send[...] = own_total[half : 2 * half].astype(BF16)
    grad_copy.start()
    grad_copy.wait_recv()
    for c in range(CHUNKS):
        home_copy(c).wait_recv()
        span = slice(c * chunk, (c + 1) * chunk)
        result = own_total[0:half, span] + own_recv[:, span].astype(F32) + home_recv[c].astype(F32)
        out[0:parts, span] = result[0:parts]
        out[parts:half_width, span] = result[pad : pad + parts]
    grad_copy.wait_send()
    for c in range(CHUNKS):
        for done in (own_copy, table_copy, forward_copy, pair_copy, home_copy):
            done(c).wait_send()


def fused(shift, n_dom, table, rel, head, tail, rid, neg, live):
    half_width, rows = table.shape
    blocks, edges = head.shape
    half = 2 * padded(half_width // 2)
    chunk = rows // CHUNKS
    steps = blocks * (edges // TILE)
    copies = 1 + 5 * CHUNKS
    vmem = pl.BlockSpec(memory_space=pltpu.VMEM)
    return pl.pallas_call(
        functools.partial(kernel, shift, n_dom),
        out_shape=jax.ShapeDtypeStruct((half_width, rows), F32),
        in_specs=[vmem] * 6 + [pl.BlockSpec(memory_space=pltpu.SMEM)],
        out_specs=vmem,
        scratch_shapes=[
            pltpu.VMEM((CHUNKS, 2 * half, chunk), BF16),
            pltpu.VMEM((CHUNKS, 2 * half, chunk), BF16),
            pltpu.VMEM((chunk, 2 * half), BF16),
            pltpu.VMEM((steps, 2 * half, TILE), BF16),
            pltpu.VMEM((steps, 2 * half, TILE), F32),
            pltpu.VMEM((steps, rows, TILE), BF16),
            pltpu.VMEM((blocks, rows, 1), F32),
            pltpu.VMEM((steps, 2 * half, TILE), F32),
            pltpu.VMEM((CHUNKS, 2 * half, chunk), F32),
            pltpu.VMEM((2 * half, rows), F32),
            pltpu.VMEM((CHUNKS, half, chunk), BF16),
            pltpu.VMEM((CHUNKS, half, chunk), BF16),
            pltpu.VMEM((CHUNKS, half, chunk), BF16),
            pltpu.VMEM((CHUNKS, half, chunk), BF16),
            pltpu.VMEM((half, rows), BF16),
            pltpu.VMEM((half, rows), BF16),
            pltpu.SemaphoreType.DMA((copies,)),
            pltpu.SemaphoreType.DMA((copies,)),
        ],
        compiler_params=pltpu.CompilerParams(
            collective_id=shift - 1, has_side_effects=True, vmem_limit_bytes=48 * 1024 * 1024
        ),
    )(table, rel, head, tail, rid, neg, live)


def local(table, rel, round_shift, head, tail, rid, neg, live):
    n_dom = lax.axis_size("dom")
    branches = [functools.partial(fused, shift, n_dom) for shift in range(1, n_dom)]
    return lax.switch(round_shift[0] - 1, branches, table.T, rel, head, tail, rid, neg, live).T


def shifted(value, axis, steps):
    count = lax.axis_size(axis)
    pairs = [(source, (source + steps) % count) for source in range(count)]
    return lax.ppermute(value, axis, pairs)


def complex_product(left_rows, right_rows, halves):
    row_shape = left_rows.shape
    split_shape = row_shape[:-1] + (halves, 2, row_shape[-1] // (2 * halves))
    left_parts = left_rows.reshape(split_shape)
    right_parts = right_rows.reshape(split_shape)
    real_part = (
        left_parts[..., 0, :] * right_parts[..., 0, :]
        - left_parts[..., 1, :] * right_parts[..., 1, :]
    )
    imag_part = (
        left_parts[..., 0, :] * right_parts[..., 1, :]
        + left_parts[..., 1, :] * right_parts[..., 0, :]
    )
    return jnp.stack([real_part, imag_part], axis=-2).reshape(row_shape)


def conjugate_product(grad_rows, right_rows, halves):
    row_shape = grad_rows.shape
    split_shape = row_shape[:-1] + (halves, 2, row_shape[-1] // (2 * halves))
    grad_parts = grad_rows.reshape(split_shape)
    right_parts = right_rows.reshape(split_shape)
    real_part = (
        grad_parts[..., 0, :] * right_parts[..., 0, :]
        + grad_parts[..., 1, :] * right_parts[..., 1, :]
    )
    imag_part = (
        grad_parts[..., 1, :] * right_parts[..., 0, :]
        - grad_parts[..., 0, :] * right_parts[..., 1, :]
    )
    return jnp.stack([real_part, imag_part], axis=-2).reshape(row_shape)


def pick_relations(ids, table):
    relation_index = jnp.arange(table.shape[0], dtype=jnp.int32)
    selector = (ids[:, None] == relation_index[None, :]).astype(jnp.float32)
    return jnp.dot(selector, table, precision=lax.Precision.HIGHEST)


def score_block(queries, tail_vectors, negative_vectors, live_count, neg_scale):
    edge_count = queries.shape[0]
    live_mask = (jnp.arange(edge_count, dtype=jnp.int32) < live_count).astype(jnp.float32)
    query_wide = queries.astype(jnp.float32)
    positive = jnp.sum(query_wide * tail_vectors.astype(jnp.float32), axis=1)
    negative = lax.dot_general(
        queries, negative_vectors, (((1,), (1,)), ((), ())), preferred_element_type=jnp.float32
    )
    tail_coef = -live_mask * jax.nn.sigmoid(-positive)
    neg_coef = (live_mask[:, None] * jax.nn.sigmoid(negative) * neg_scale).astype(jnp.bfloat16)
    grad_query = (
        tail_coef[:, None] * tail_vectors.astype(jnp.float32)
        + jnp.dot(neg_coef, negative_vectors, preferred_element_type=jnp.float32)
    ).astype(jnp.bfloat16)
    neg_grad = lax.dot_general(
        neg_coef, queries, (((0,), (0,)), ((), ())), preferred_element_type=jnp.float32
    )
    return (grad_query, tail_coef[:, None] * query_wide, neg_grad)


def local_hops(
    entity_table,
    relation_table,
    round_shift,
    head_rows,
    tail_rows,
    relation_ids,
    negative_rows,
    live_edges,
):
    row_count = entity_table.shape[0]
    full_width = relation_table.shape[1]
    halves = lax.axis_size("shard")
    block_count = head_rows.shape[0]
    neg_scale = negative_rows.shape[1] ** (-0.5)
    hop_count = (lax.axis_size("dom") - 1).bit_length()
    offset = round_shift[0]
    own_low = entity_table.astype(jnp.bfloat16)
    own_table = lax.all_gather(own_low, "shard", axis=1, tiled=True)
    relation_list = [
        pick_relations(relation_ids[block_index], relation_table)
        for block_index in range(block_count)
    ]
    partner_grad = jnp.zeros((row_count, full_width), jnp.float32)
    partner_half = own_low
    for bit_index in range(hop_count):
        arrived = shifted(partner_half, "dom", -(1 << bit_index))
        take_hop = offset // (1 << bit_index) % 2 == 1
        partner_half = jnp.where(take_hop, arrived, partner_half)
    partner_table = lax.all_gather(partner_half, "shard", axis=1, tiled=True)
    grad_list = []
    for block_index in range(block_count):
        head_vectors = own_table[head_rows[block_index]].astype(jnp.float32)
        queries = complex_product(head_vectors, relation_list[block_index], halves).astype(
            jnp.bfloat16
        )
        grad_query, tail_grad, neg_grad = score_block(
            queries,
            partner_table[tail_rows[block_index]],
            partner_table[negative_rows[block_index]],
            live_edges[block_index],
            neg_scale,
        )
        partner_grad = partner_grad.at[tail_rows[block_index]].add(tail_grad)
        partner_grad = partner_grad.at[negative_rows[block_index]].add(neg_grad)
        grad_list.append(grad_query)
    returned = jnp.stack(grad_list)
    own_grad = jnp.zeros((row_count, full_width), jnp.float32)
    for block_index in range(block_count):
        own_grad = own_grad.at[head_rows[block_index]].add(
            conjugate_product(
                returned[block_index].astype(jnp.float32), relation_list[block_index], halves
            )
        )
    partner_sum, own_sum = (
        lax.psum_scatter(partner_grad, "shard", scatter_dimension=1, tiled=True),
        lax.psum_scatter(own_grad, "shard", scatter_dimension=1, tiled=True),
    )
    going_back = partner_sum.astype(jnp.bfloat16)
    for bit_index in range(hop_count):
        arrived = shifted(going_back, "dom", 1 << bit_index)
        take_hop = offset // (1 << bit_index) % 2 == 1
        going_back = jnp.where(take_hop, arrived, going_back)
    return own_sum + going_back.astype(jnp.float32)


def solution(mesh):
    in_specs = (
        P(("groups", "dom"), "shard"),
        P("groups", None),
        P(),
        P(("groups", "dom", "shard"), None),
        P(("groups", "dom", "shard"), None),
        P(("groups", "dom", "shard"), None),
        P(("groups", "dom", "shard"), None),
        P(("groups", "dom", "shard")),
    )
    out_specs = P(("groups", "dom"), "shard")
    return jax.shard_map(
        local if mesh.shape["dom"] <= 8 else local_hops,
        mesh=mesh, in_specs=in_specs, out_specs=out_specs, check_vma=False)
```

```python
import functools

import jax
import jax.numpy as jnp
from jax import lax
from jax.experimental import pallas as pl
from jax.experimental.pallas import tpu as pltpu
from jax.sharding import PartitionSpec as P

MESH = pl.DeviceIdType.MESH
BF16 = jnp.bfloat16
F32 = jnp.float32
NN = (((1,), (0,)), ((), ()))
NT = (((1,), (1,)), ((), ()))
TN = (((0,), (0,)), ((), ()))
CHUNKS = 2
TILE = 1024


def mm(left, right, dims):
    return lax.dot_general(left, right, dims, preferred_element_type=F32)


def padded(parts):
    return -(-parts // 8) * 8


def select_columns(parts, width, first):
    pad = padded(parts)
    row = lax.broadcasted_iota(jnp.int32, (2 * pad, width), 0)
    col = lax.broadcasted_iota(jnp.int32, (2 * pad, width), 1) - first
    real = (row < parts) & (col == row)
    imag = (row >= pad) & (row < pad + parts) & (col == row - pad + parts)
    return jnp.where(real | imag, 1.0, 0.0).astype(BF16)


def one_hot(ids, count, first=0, modulus=None):
    row = lax.broadcasted_iota(jnp.int32, (count, ids.shape[1]), 0)
    if modulus is not None:
        row = jnp.where(row >= modulus, row - modulus, row)
    return row + first == ids


def kernel(
    shift, n_dom, table, rel, head, tail, rid, neg, live, out,
    own, part, query, rel_edge, hot, count, coef, total, own_total,
    pair_send, pair_recv, home_send, home_recv, own_send, own_recv, send_sem, recv_sem,
):
    half_width, rows = table.shape
    parts = half_width // 2
    pad = padded(parts)
    half = 2 * pad
    blocks, edges = head.shape
    relations = rel.shape[0]
    chunk = rows // CHUNKS
    tiles = edges // TILE
    scale = 0.5 * neg.shape[1] ** (-0.5)
    side = lax.axis_index("shard")
    me = lax.axis_index("dom")
    mate = {"shard": 1 - side}
    asker = {"dom": lax.rem(me + n_dom - shift, n_dom)}
    partner = {"dom": lax.rem(me + shift, n_dom)}

    def copy(index, source, target, device):
        return pltpu.make_async_remote_copy(
            src_ref=source, dst_ref=target, send_sem=send_sem.at[index],
            recv_sem=recv_sem.at[index], device_id=device, device_id_type=MESH,
        )

    barrier = pltpu.get_barrier_semaphore()
    for device in (mate, asker, partner):
        pl.semaphore_signal(barrier, inc=1, device_id=device, device_id_type=MESH)
    choose = select_columns(parts, half_width, 0)
    mine = mm(choose, table[...].astype(BF16), NN).astype(BF16)
    own[0:half] = mine
    pl.semaphore_wait(barrier, 3)

    low_half, high_half = pl.ds(0, half), pl.ds(half, half)

    def rows_of(c):
        return pl.ds(pl.multiple_of(c * chunk, chunk), chunk)

    def table_copy(c):
        return copy(c, own.at[low_half, rows_of(c)], part.at[low_half, rows_of(c)], asker)

    def forward_copy(c):
        return copy(CHUNKS + c, part.at[low_half, rows_of(c)], part.at[high_half, rows_of(c)], mate)

    def pair_copy(c):
        return copy(2 * CHUNKS + c, pair_send.at[c], pair_recv.at[c], mate)

    def home_copy(c):
        return copy(3 * CHUNKS + c, home_send.at[c], home_recv.at[c], partner)

    grad_copy = copy(4 * CHUNKS, own_send, own_recv, mate)
    own_copy = copy(4 * CHUNKS + 1, own.at[low_half], own.at[high_half], mate)
    table_copy(0).start()
    own_copy.start()
    for c in range(1, CHUNKS):
        table_copy(c).start()

    wide = rel[...]
    high = wide.astype(BF16)
    low = (wide - high.astype(F32)).astype(BF16)
    pieces = jnp.concatenate([high, low], axis=0)
    choose_all = jnp.concatenate(
        [
            select_columns(parts, 2 * half_width, side * half_width),
            select_columns(parts, 2 * half_width, (1 - side) * half_width),
        ],
        axis=0,
    )
    rel_rows = mm(choose_all, pieces, NT).astype(BF16)
    count[...] = jnp.zeros_like(count)

    def place(t):
        b = t // tiles
        first = pl.multiple_of((t - b * tiles) * TILE, TILE)
        return b, first

    def index_step(t, _):
        b, first = place(t)
        spot = (pl.ds(b, 1), pl.ds(first, TILE))
        pick = jnp.where(one_hot(rid[spot], 2 * relations, 0, relations), 1.0, 0.0).astype(BF16)
        rel_edge[t] = mm(rel_rows, pick, NN)
        edge_index = first + lax.broadcasted_iota(jnp.int32, (1, TILE), 1)
        live_head = jnp.where(edge_index < live[b], head[spot], -1)
        hot[t] = jnp.where(one_hot(live_head, rows), 1.0, 0.0).astype(BF16)
        seen = jnp.where(one_hot(neg[spot], rows), scale, 0.0)
        count[b] = count[b] + jnp.sum(seen, axis=1, keepdims=True)
        return 0

    lax.fori_loop(0, blocks * tiles, index_step, 0)
    own_copy.wait_recv()

    def forward(c):
        table_copy(c).wait_recv()
        forward_copy(c).start()

    def query_step(t, _):
        heads = mm(own[...], hot[t], NN)
        for j in range(2):
            real, imag = j * half, j * half + pad
            h_re, h_im = heads[real:imag], heads[imag : imag + pad]
            r_re, r_im = rel_edge[t, real:imag], rel_edge[t, imag : imag + pad]
            query[t, real : real + half] = jnp.concatenate(
                [h_re * r_re - h_im * r_im, h_re * r_im + h_im * r_re], axis=0
            ).astype(BF16)

        @pl.when(t == 0)
        def _():
            forward(0)

        return 0

    lax.fori_loop(0, blocks * tiles, query_step, 0)

    def send_home(c):
        pair_copy(c).wait_recv()
        home_send[c] = (total[c, 0:half] + pair_recv[c].astype(F32)).astype(BF16)
        home_copy(c).start()

    row_index = lax.broadcasted_iota(jnp.int32, (chunk, chunk), 0)
    col_index = lax.broadcasted_iota(jnp.int32, (chunk, chunk), 1)
    same = jnp.where(row_index == col_index, 1.0, 0.0).astype(BF16)

    def chunk_step(c, _):
        @pl.when(c + 1 < CHUNKS)
        def _():
            forward(c + 1)

        forward_copy(c).wait_recv()
        part_rows = mm(same, part[:, rows_of(c)], NT).astype(BF16)
        total[c] = jnp.zeros_like(total[c])
        start = pl.multiple_of(c * chunk, chunk)

        def score_step(t, _):
            b, first = place(t)
            score = mm(part_rows, query[t], NN)
            curve = jnp.tanh(0.5 * score)
            ids = tail[pl.ds(b, 1), pl.ds(first, TILE)]
            at_tail = jnp.where(one_hot(ids, chunk, start), 0.5, 0.0)
            weight = count[b, pl.ds(start, chunk)]
            step = ((weight - at_tail) + curve * (weight + at_tail)).astype(BF16)
            coef[t, rows_of(c)] = step
            total[c] = total[c] + mm(query[t], step, NT)
            return 0

        lax.fori_loop(0, blocks * tiles, score_step, 0)
        pair_send[c] = total[c, half : 2 * half].astype(BF16)
        pair_copy(c).start()

        @pl.when(c > 0)
        def _():
            send_home(c - 1)

        return 0

    lax.fori_loop(0, CHUNKS, chunk_step, 0)
    own_total[...] = jnp.zeros_like(own_total)

    def own_step(t, _):
        halves = []
        grad_query = mm(part[...], coef[t], NN)
        for j in range(2):
            real, imag = j * half, j * half + pad
            grads = grad_query[real : real + half].astype(BF16).astype(F32)
            g_re, g_im = grads[0:pad], grads[pad:half]
            r_re, r_im = rel_edge[t, real:imag], rel_edge[t, imag : imag + pad]
            halves += [g_re * r_re + g_im * r_im, g_im * r_re - g_re * r_im]
        own_total[...] = own_total[...] + mm(jnp.concatenate(halves, axis=0).astype(BF16), hot[t], NT)

        @pl.when(t == 0)
        def _():
            send_home(CHUNKS - 1)

        return 0

    lax.fori_loop(0, blocks * tiles, own_step, 0)
    own_send[...] = own_total[half : 2 * half].astype(BF16)
    grad_copy.start()
    grad_copy.wait_recv()
    for c in range(CHUNKS):
        home_copy(c).wait_recv()
        span = slice(c * chunk, (c + 1) * chunk)
        result = own_total[0:half, span] + own_recv[:, span].astype(F32) + home_recv[c].astype(F32)
        out[0:parts, span] = result[0:parts]
        out[parts:half_width, span] = result[pad : pad + parts]
    grad_copy.wait_send()
    own_copy.wait_send()
    for c in range(CHUNKS):
        for done in (table_copy, forward_copy, pair_copy, home_copy):
            done(c).wait_send()


def fused(shift, n_dom, table, rel, head, tail, rid, neg, live):
    half_width, rows = table.shape
    blocks, edges = head.shape
    half = 2 * padded(half_width // 2)
    chunk = rows // CHUNKS
    steps = blocks * (edges // TILE)
    copies = 2 + 4 * CHUNKS
    vmem = pl.BlockSpec(memory_space=pltpu.VMEM)
    return pl.pallas_call(
        functools.partial(kernel, shift, n_dom),
        out_shape=jax.ShapeDtypeStruct((half_width, rows), F32),
        in_specs=[vmem] * 6 + [pl.BlockSpec(memory_space=pltpu.SMEM)],
        out_specs=vmem,
        scratch_shapes=[
            pltpu.VMEM((2 * half, rows), BF16),
            pltpu.VMEM((2 * half, rows), BF16),
            pltpu.VMEM((steps, 2 * half, TILE), BF16),
            pltpu.VMEM((steps, 2 * half, TILE), F32),
            pltpu.VMEM((steps, rows, TILE), BF16),
            pltpu.VMEM((blocks, rows, 1), F32),
            pltpu.VMEM((steps, rows, TILE), BF16),
            pltpu.VMEM((CHUNKS, 2 * half, chunk), F32),
            pltpu.VMEM((2 * half, rows), F32),
            pltpu.VMEM((CHUNKS, half, chunk), BF16),
            pltpu.VMEM((CHUNKS, half, chunk), BF16),
            pltpu.VMEM((CHUNKS, half, chunk), BF16),
            pltpu.VMEM((CHUNKS, half, chunk), BF16),
            pltpu.VMEM((half, rows), BF16),
            pltpu.VMEM((half, rows), BF16),
            pltpu.SemaphoreType.DMA((copies,)),
            pltpu.SemaphoreType.DMA((copies,)),
        ],
        compiler_params=pltpu.CompilerParams(
            collective_id=shift - 1, has_side_effects=True, vmem_limit_bytes=48 * 1024 * 1024
        ),
    )(table, rel, head, tail, rid, neg, live)


def local(table, rel, round_shift, head, tail, rid, neg, live):
    n_dom = lax.axis_size("dom")
    branches = [functools.partial(fused, shift, n_dom) for shift in range(1, n_dom)]
    return lax.switch(round_shift[0] - 1, branches, table.T, rel, head, tail, rid, neg, live).T


def shifted(value, axis, steps):
    count = lax.axis_size(axis)
    pairs = [(source, (source + steps) % count) for source in range(count)]
    return lax.ppermute(value, axis, pairs)


def complex_product(left_rows, right_rows, halves):
    row_shape = left_rows.shape
    split_shape = row_shape[:-1] + (halves, 2, row_shape[-1] // (2 * halves))
    left_parts = left_rows.reshape(split_shape)
    right_parts = right_rows.reshape(split_shape)
    real_part = (
        left_parts[..., 0, :] * right_parts[..., 0, :]
        - left_parts[..., 1, :] * right_parts[..., 1, :]
    )
    imag_part = (
        left_parts[..., 0, :] * right_parts[..., 1, :]
        + left_parts[..., 1, :] * right_parts[..., 0, :]
    )
    return jnp.stack([real_part, imag_part], axis=-2).reshape(row_shape)


def conjugate_product(grad_rows, right_rows, halves):
    row_shape = grad_rows.shape
    split_shape = row_shape[:-1] + (halves, 2, row_shape[-1] // (2 * halves))
    grad_parts = grad_rows.reshape(split_shape)
    right_parts = right_rows.reshape(split_shape)
    real_part = (
        grad_parts[..., 0, :] * right_parts[..., 0, :]
        + grad_parts[..., 1, :] * right_parts[..., 1, :]
    )
    imag_part = (
        grad_parts[..., 1, :] * right_parts[..., 0, :]
        - grad_parts[..., 0, :] * right_parts[..., 1, :]
    )
    return jnp.stack([real_part, imag_part], axis=-2).reshape(row_shape)


def pick_relations(ids, table):
    relation_index = jnp.arange(table.shape[0], dtype=jnp.int32)
    selector = (ids[:, None] == relation_index[None, :]).astype(jnp.float32)
    return jnp.dot(selector, table, precision=lax.Precision.HIGHEST)


def score_block(queries, tail_vectors, negative_vectors, live_count, neg_scale):
    edge_count = queries.shape[0]
    live_mask = (jnp.arange(edge_count, dtype=jnp.int32) < live_count).astype(jnp.float32)
    query_wide = queries.astype(jnp.float32)
    positive = jnp.sum(query_wide * tail_vectors.astype(jnp.float32), axis=1)
    negative = lax.dot_general(
        queries, negative_vectors, (((1,), (1,)), ((), ())), preferred_element_type=jnp.float32
    )
    tail_coef = -live_mask * jax.nn.sigmoid(-positive)
    neg_coef = (live_mask[:, None] * jax.nn.sigmoid(negative) * neg_scale).astype(jnp.bfloat16)
    grad_query = (
        tail_coef[:, None] * tail_vectors.astype(jnp.float32)
        + jnp.dot(neg_coef, negative_vectors, preferred_element_type=jnp.float32)
    ).astype(jnp.bfloat16)
    neg_grad = lax.dot_general(
        neg_coef, queries, (((0,), (0,)), ((), ())), preferred_element_type=jnp.float32
    )
    return (grad_query, tail_coef[:, None] * query_wide, neg_grad)


def local_hops(
    entity_table,
    relation_table,
    round_shift,
    head_rows,
    tail_rows,
    relation_ids,
    negative_rows,
    live_edges,
):
    row_count = entity_table.shape[0]
    full_width = relation_table.shape[1]
    halves = lax.axis_size("shard")
    block_count = head_rows.shape[0]
    neg_scale = negative_rows.shape[1] ** (-0.5)
    hop_count = (lax.axis_size("dom") - 1).bit_length()
    offset = round_shift[0]
    own_low = entity_table.astype(jnp.bfloat16)
    own_table = lax.all_gather(own_low, "shard", axis=1, tiled=True)
    relation_list = [
        pick_relations(relation_ids[block_index], relation_table)
        for block_index in range(block_count)
    ]
    partner_grad = jnp.zeros((row_count, full_width), jnp.float32)
    partner_half = own_low
    for bit_index in range(hop_count):
        arrived = shifted(partner_half, "dom", -(1 << bit_index))
        take_hop = offset // (1 << bit_index) % 2 == 1
        partner_half = jnp.where(take_hop, arrived, partner_half)
    partner_table = lax.all_gather(partner_half, "shard", axis=1, tiled=True)
    grad_list = []
    for block_index in range(block_count):
        head_vectors = own_table[head_rows[block_index]].astype(jnp.float32)
        queries = complex_product(head_vectors, relation_list[block_index], halves).astype(
            jnp.bfloat16
        )
        grad_query, tail_grad, neg_grad = score_block(
            queries,
            partner_table[tail_rows[block_index]],
            partner_table[negative_rows[block_index]],
            live_edges[block_index],
            neg_scale,
        )
        partner_grad = partner_grad.at[tail_rows[block_index]].add(tail_grad)
        partner_grad = partner_grad.at[negative_rows[block_index]].add(neg_grad)
        grad_list.append(grad_query)
    returned = jnp.stack(grad_list)
    own_grad = jnp.zeros((row_count, full_width), jnp.float32)
    for block_index in range(block_count):
        own_grad = own_grad.at[head_rows[block_index]].add(
            conjugate_product(
                returned[block_index].astype(jnp.float32), relation_list[block_index], halves
            )
        )
    partner_sum, own_sum = (
        lax.psum_scatter(partner_grad, "shard", scatter_dimension=1, tiled=True),
        lax.psum_scatter(own_grad, "shard", scatter_dimension=1, tiled=True),
    )
    going_back = partner_sum.astype(jnp.bfloat16)
    for bit_index in range(hop_count):
        arrived = shifted(going_back, "dom", 1 << bit_index)
        take_hop = offset // (1 << bit_index) % 2 == 1
        going_back = jnp.where(take_hop, arrived, going_back)
    return own_sum + going_back.astype(jnp.float32)


def solution(mesh):
    in_specs = (
        P(("groups", "dom"), "shard"),
        P("groups", None),
        P(),
        P(("groups", "dom", "shard"), None),
        P(("groups", "dom", "shard"), None),
        P(("groups", "dom", "shard"), None),
        P(("groups", "dom", "shard"), None),
        P(("groups", "dom", "shard")),
    )
    out_specs = P(("groups", "dom"), "shard")
    return jax.shard_map(
        local if mesh.shape["dom"] <= 8 else local_hops,
        mesh=mesh, in_specs=in_specs, out_specs=out_specs, check_vma=False)
```

```python
import functools

import jax
import jax.numpy as jnp
from jax import lax
from jax.experimental import pallas as pl
from jax.experimental.pallas import tpu as pltpu
from jax.sharding import PartitionSpec as P

MESH = pl.DeviceIdType.MESH
BF16 = jnp.bfloat16
F32 = jnp.float32
NN = (((1,), (0,)), ((), ()))
NT = (((1,), (1,)), ((), ()))
TN = (((0,), (0,)), ((), ()))
CHUNKS = 2
TILE = 1024


def mm(left, right, dims):
    return lax.dot_general(left, right, dims, preferred_element_type=F32)


def padded(parts):
    return -(-parts // 8) * 8


def select_columns(parts, width, first):
    pad = padded(parts)
    row = lax.broadcasted_iota(jnp.int32, (2 * pad, width), 0)
    col = lax.broadcasted_iota(jnp.int32, (2 * pad, width), 1) - first
    real = (row < parts) & (col == row)
    imag = (row >= pad) & (row < pad + parts) & (col == row - pad + parts)
    return jnp.where(real | imag, 1.0, 0.0).astype(BF16)


def one_hot(ids, count, first=0, modulus=None):
    row = lax.broadcasted_iota(jnp.int32, (count, ids.shape[1]), 0)
    if modulus is not None:
        row = jnp.where(row >= modulus, row - modulus, row)
    return row + first == ids


def kernel(
    shift, n_dom, table, rel, head, tail, rid, neg, live, out,
    own, part, query, rel_edge, hot, count, coef, total, own_total,
    pair_send, pair_recv, home_send, home_recv, own_send, own_recv, send_sem, recv_sem,
):
    half_width, rows = table.shape
    parts = half_width // 2
    pad = padded(parts)
    half = 2 * pad
    blocks, edges = head.shape
    relations = rel.shape[0]
    chunk = rows // CHUNKS
    tiles = edges // TILE
    scale = 0.5 * neg.shape[1] ** (-0.5)
    side = lax.axis_index("shard")
    me = lax.axis_index("dom")
    mate = {"shard": 1 - side}
    asker = {"dom": lax.rem(me + n_dom - shift, n_dom)}
    partner = {"dom": lax.rem(me + shift, n_dom)}

    def copy(index, source, target, device):
        return pltpu.make_async_remote_copy(
            src_ref=source, dst_ref=target, send_sem=send_sem.at[index],
            recv_sem=recv_sem.at[index], device_id=device, device_id_type=MESH,
        )

    barrier = pltpu.get_barrier_semaphore()
    for device in (mate, asker, partner):
        pl.semaphore_signal(barrier, inc=1, device_id=device, device_id_type=MESH)
    choose = select_columns(parts, half_width, 0)
    mine = mm(choose, table[...].astype(BF16), NN).astype(BF16)
    own[0:half] = mine
    pl.semaphore_wait(barrier, 3)

    low_half, high_half = pl.ds(0, half), pl.ds(half, half)

    def rows_of(c):
        return pl.ds(pl.multiple_of(c * chunk, chunk), chunk)

    def table_copy(c):
        return copy(c, own.at[low_half, rows_of(c)], part.at[low_half, rows_of(c)], asker)

    def forward_copy(c):
        return copy(CHUNKS + c, part.at[low_half, rows_of(c)], part.at[high_half, rows_of(c)], mate)

    def pair_copy(c):
        return copy(2 * CHUNKS + c, pair_send.at[c], pair_recv.at[c], mate)

    def home_copy(c):
        return copy(3 * CHUNKS + c, home_send.at[c], home_recv.at[c], partner)

    grad_copy = copy(4 * CHUNKS, own_send, own_recv, mate)
    own_copy = copy(4 * CHUNKS + 1, own.at[low_half], own.at[high_half], mate)
    table_copy(0).start()
    own_copy.start()

    wide = rel[...]
    high = wide.astype(BF16)
    low = (wide - high.astype(F32)).astype(BF16)
    pieces = jnp.concatenate([high, low], axis=0)
    choose_all = jnp.concatenate(
        [
            select_columns(parts, 2 * half_width, side * half_width),
            select_columns(parts, 2 * half_width, (1 - side) * half_width),
        ],
        axis=0,
    )
    rel_rows = mm(choose_all, pieces, NT).astype(BF16)
    count[...] = jnp.zeros_like(count)

    def place(t):
        b = t // tiles
        first = pl.multiple_of((t - b * tiles) * TILE, TILE)
        return b, first

    def index_step(t, _):
        b, first = place(t)
        spot = (pl.ds(b, 1), pl.ds(first, TILE))
        pick = jnp.where(one_hot(rid[spot], 2 * relations, 0, relations), 1.0, 0.0).astype(BF16)
        rel_edge[t] = mm(rel_rows, pick, NN)
        edge_index = first + lax.broadcasted_iota(jnp.int32, (1, TILE), 1)
        live_head = jnp.where(edge_index < live[b], head[spot], -1)
        hot[t] = jnp.where(one_hot(live_head, rows), 1.0, 0.0).astype(BF16)
        seen = jnp.where(one_hot(neg[spot], rows), scale, 0.0)
        count[b] = count[b] + jnp.sum(seen, axis=1, keepdims=True)
        return 0

    lax.fori_loop(0, blocks * tiles, index_step, 0)
    for c in range(1, CHUNKS):
        table_copy(c).start()
    own_copy.wait_recv()

    def forward(c):
        table_copy(c).wait_recv()
        forward_copy(c).start()

    def query_step(t, _):
        heads = mm(own[...], hot[t], NN)
        for j in range(2):
            real, imag = j * half, j * half + pad
            h_re, h_im = heads[real:imag], heads[imag : imag + pad]
            r_re, r_im = rel_edge[t, real:imag], rel_edge[t, imag : imag + pad]
            query[t, real : real + half] = jnp.concatenate(
                [h_re * r_re - h_im * r_im, h_re * r_im + h_im * r_re], axis=0
            ).astype(BF16)

        @pl.when(t == 0)
        def _():
            forward(0)

        return 0

    lax.fori_loop(0, blocks * tiles, query_step, 0)

    def send_home(c):
        pair_copy(c).wait_recv()
        home_send[c] = (total[c, 0:half] + pair_recv[c].astype(F32)).astype(BF16)
        home_copy(c).start()

    row_index = lax.broadcasted_iota(jnp.int32, (chunk, chunk), 0)
    col_index = lax.broadcasted_iota(jnp.int32, (chunk, chunk), 1)
    same = jnp.where(row_index == col_index, 1.0, 0.0).astype(BF16)

    def chunk_step(c, _):
        @pl.when(c + 1 < CHUNKS)
        def _():
            forward(c + 1)

        forward_copy(c).wait_recv()
        part_rows = mm(same, part[:, rows_of(c)], NT).astype(BF16)
        total[c] = jnp.zeros_like(total[c])
        start = pl.multiple_of(c * chunk, chunk)

        def score_step(t, _):
            b, first = place(t)
            score = mm(part_rows, query[t], NN)
            curve = jnp.tanh(0.5 * score)
            ids = tail[pl.ds(b, 1), pl.ds(first, TILE)]
            at_tail = jnp.where(one_hot(ids, chunk, start), 0.5, 0.0)
            weight = count[b, pl.ds(start, chunk)]
            step = ((weight - at_tail) + curve * (weight + at_tail)).astype(BF16)
            coef[t, rows_of(c)] = step
            total[c] = total[c] + mm(query[t], step, NT)

            @pl.when((t == 0) & (c > 0))
            def _():
                send_home(c - 1)

            return 0

        lax.fori_loop(0, blocks * tiles, score_step, 0)
        pair_send[c] = total[c, half : 2 * half].astype(BF16)
        pair_copy(c).start()
        return 0

    lax.fori_loop(0, CHUNKS, chunk_step, 0)
    own_total[...] = jnp.zeros_like(own_total)

    def own_step(t, _):
        halves = []
        grad_query = mm(part[...], coef[t], NN)
        for j in range(2):
            real, imag = j * half, j * half + pad
            grads = grad_query[real : real + half].astype(BF16).astype(F32)
            g_re, g_im = grads[0:pad], grads[pad:half]
            r_re, r_im = rel_edge[t, real:imag], rel_edge[t, imag : imag + pad]
            halves += [g_re * r_re + g_im * r_im, g_im * r_re - g_re * r_im]
        own_total[...] = own_total[...] + mm(jnp.concatenate(halves, axis=0).astype(BF16), hot[t], NT)

        @pl.when(t == 0)
        def _():
            send_home(CHUNKS - 1)

        return 0

    lax.fori_loop(0, blocks * tiles, own_step, 0)
    own_send[...] = own_total[half : 2 * half].astype(BF16)
    grad_copy.start()
    grad_copy.wait_recv()
    for c in range(CHUNKS):
        home_copy(c).wait_recv()
        span = slice(c * chunk, (c + 1) * chunk)
        result = own_total[0:half, span] + own_recv[:, span].astype(F32) + home_recv[c].astype(F32)
        out[0:parts, span] = result[0:parts]
        out[parts:half_width, span] = result[pad : pad + parts]
    grad_copy.wait_send()
    own_copy.wait_send()
    for c in range(CHUNKS):
        for done in (table_copy, forward_copy, pair_copy, home_copy):
            done(c).wait_send()


def fused(shift, n_dom, table, rel, head, tail, rid, neg, live):
    half_width, rows = table.shape
    blocks, edges = head.shape
    half = 2 * padded(half_width // 2)
    chunk = rows // CHUNKS
    steps = blocks * (edges // TILE)
    copies = 2 + 4 * CHUNKS
    vmem = pl.BlockSpec(memory_space=pltpu.VMEM)
    return pl.pallas_call(
        functools.partial(kernel, shift, n_dom),
        out_shape=jax.ShapeDtypeStruct((half_width, rows), F32),
        in_specs=[vmem] * 6 + [pl.BlockSpec(memory_space=pltpu.SMEM)],
        out_specs=vmem,
        scratch_shapes=[
            pltpu.VMEM((2 * half, rows), BF16),
            pltpu.VMEM((2 * half, rows), BF16),
            pltpu.VMEM((steps, 2 * half, TILE), BF16),
            pltpu.VMEM((steps, 2 * half, TILE), F32),
            pltpu.VMEM((steps, rows, TILE), BF16),
            pltpu.VMEM((blocks, rows, 1), F32),
            pltpu.VMEM((steps, rows, TILE), BF16),
            pltpu.VMEM((CHUNKS, 2 * half, chunk), F32),
            pltpu.VMEM((2 * half, rows), F32),
            pltpu.VMEM((CHUNKS, half, chunk), BF16),
            pltpu.VMEM((CHUNKS, half, chunk), BF16),
            pltpu.VMEM((CHUNKS, half, chunk), BF16),
            pltpu.VMEM((CHUNKS, half, chunk), BF16),
            pltpu.VMEM((half, rows), BF16),
            pltpu.VMEM((half, rows), BF16),
            pltpu.SemaphoreType.DMA((copies,)),
            pltpu.SemaphoreType.DMA((copies,)),
        ],
        compiler_params=pltpu.CompilerParams(
            collective_id=shift - 1, has_side_effects=True, vmem_limit_bytes=48 * 1024 * 1024
        ),
    )(table, rel, head, tail, rid, neg, live)


def local(table, rel, round_shift, head, tail, rid, neg, live):
    n_dom = lax.axis_size("dom")
    branches = [functools.partial(fused, shift, n_dom) for shift in range(1, n_dom)]
    return lax.switch(round_shift[0] - 1, branches, table.T, rel, head, tail, rid, neg, live).T


def shifted(value, axis, steps):
    count = lax.axis_size(axis)
    pairs = [(source, (source + steps) % count) for source in range(count)]
    return lax.ppermute(value, axis, pairs)


def complex_product(left_rows, right_rows, halves):
    row_shape = left_rows.shape
    split_shape = row_shape[:-1] + (halves, 2, row_shape[-1] // (2 * halves))
    left_parts = left_rows.reshape(split_shape)
    right_parts = right_rows.reshape(split_shape)
    real_part = (
        left_parts[..., 0, :] * right_parts[..., 0, :]
        - left_parts[..., 1, :] * right_parts[..., 1, :]
    )
    imag_part = (
        left_parts[..., 0, :] * right_parts[..., 1, :]
        + left_parts[..., 1, :] * right_parts[..., 0, :]
    )
    return jnp.stack([real_part, imag_part], axis=-2).reshape(row_shape)


def conjugate_product(grad_rows, right_rows, halves):
    row_shape = grad_rows.shape
    split_shape = row_shape[:-1] + (halves, 2, row_shape[-1] // (2 * halves))
    grad_parts = grad_rows.reshape(split_shape)
    right_parts = right_rows.reshape(split_shape)
    real_part = (
        grad_parts[..., 0, :] * right_parts[..., 0, :]
        + grad_parts[..., 1, :] * right_parts[..., 1, :]
    )
    imag_part = (
        grad_parts[..., 1, :] * right_parts[..., 0, :]
        - grad_parts[..., 0, :] * right_parts[..., 1, :]
    )
    return jnp.stack([real_part, imag_part], axis=-2).reshape(row_shape)


def pick_relations(ids, table):
    relation_index = jnp.arange(table.shape[0], dtype=jnp.int32)
    selector = (ids[:, None] == relation_index[None, :]).astype(jnp.float32)
    return jnp.dot(selector, table, precision=lax.Precision.HIGHEST)


def score_block(queries, tail_vectors, negative_vectors, live_count, neg_scale):
    edge_count = queries.shape[0]
    live_mask = (jnp.arange(edge_count, dtype=jnp.int32) < live_count).astype(jnp.float32)
    query_wide = queries.astype(jnp.float32)
    positive = jnp.sum(query_wide * tail_vectors.astype(jnp.float32), axis=1)
    negative = lax.dot_general(
        queries, negative_vectors, (((1,), (1,)), ((), ())), preferred_element_type=jnp.float32
    )
    tail_coef = -live_mask * jax.nn.sigmoid(-positive)
    neg_coef = (live_mask[:, None] * jax.nn.sigmoid(negative) * neg_scale).astype(jnp.bfloat16)
    grad_query = (
        tail_coef[:, None] * tail_vectors.astype(jnp.float32)
        + jnp.dot(neg_coef, negative_vectors, preferred_element_type=jnp.float32)
    ).astype(jnp.bfloat16)
    neg_grad = lax.dot_general(
        neg_coef, queries, (((0,), (0,)), ((), ())), preferred_element_type=jnp.float32
    )
    return (grad_query, tail_coef[:, None] * query_wide, neg_grad)


def local_hops(
    entity_table,
    relation_table,
    round_shift,
    head_rows,
    tail_rows,
    relation_ids,
    negative_rows,
    live_edges,
):
    row_count = entity_table.shape[0]
    full_width = relation_table.shape[1]
    halves = lax.axis_size("shard")
    block_count = head_rows.shape[0]
    neg_scale = negative_rows.shape[1] ** (-0.5)
    hop_count = (lax.axis_size("dom") - 1).bit_length()
    offset = round_shift[0]
    own_low = entity_table.astype(jnp.bfloat16)
    own_table = lax.all_gather(own_low, "shard", axis=1, tiled=True)
    relation_list = [
        pick_relations(relation_ids[block_index], relation_table)
        for block_index in range(block_count)
    ]
    partner_grad = jnp.zeros((row_count, full_width), jnp.float32)
    partner_half = own_low
    for bit_index in range(hop_count):
        arrived = shifted(partner_half, "dom", -(1 << bit_index))
        take_hop = offset // (1 << bit_index) % 2 == 1
        partner_half = jnp.where(take_hop, arrived, partner_half)
    partner_table = lax.all_gather(partner_half, "shard", axis=1, tiled=True)
    grad_list = []
    for block_index in range(block_count):
        head_vectors = own_table[head_rows[block_index]].astype(jnp.float32)
        queries = complex_product(head_vectors, relation_list[block_index], halves).astype(
            jnp.bfloat16
        )
        grad_query, tail_grad, neg_grad = score_block(
            queries,
            partner_table[tail_rows[block_index]],
            partner_table[negative_rows[block_index]],
            live_edges[block_index],
            neg_scale,
        )
        partner_grad = partner_grad.at[tail_rows[block_index]].add(tail_grad)
        partner_grad = partner_grad.at[negative_rows[block_index]].add(neg_grad)
        grad_list.append(grad_query)
    returned = jnp.stack(grad_list)
    own_grad = jnp.zeros((row_count, full_width), jnp.float32)
    for block_index in range(block_count):
        own_grad = own_grad.at[head_rows[block_index]].add(
            conjugate_product(
                returned[block_index].astype(jnp.float32), relation_list[block_index], halves
            )
        )
    partner_sum, own_sum = (
        lax.psum_scatter(partner_grad, "shard", scatter_dimension=1, tiled=True),
        lax.psum_scatter(own_grad, "shard", scatter_dimension=1, tiled=True),
    )
    going_back = partner_sum.astype(jnp.bfloat16)
    for bit_index in range(hop_count):
        arrived = shifted(going_back, "dom", 1 << bit_index)
        take_hop = offset // (1 << bit_index) % 2 == 1
        going_back = jnp.where(take_hop, arrived, going_back)
    return own_sum + going_back.astype(jnp.float32)


def solution(mesh):
    in_specs = (
        P(("groups", "dom"), "shard"),
        P("groups", None),
        P(),
        P(("groups", "dom", "shard"), None),
        P(("groups", "dom", "shard"), None),
        P(("groups", "dom", "shard"), None),
        P(("groups", "dom", "shard"), None),
        P(("groups", "dom", "shard")),
    )
    out_specs = P(("groups", "dom"), "shard")
    return jax.shard_map(
        local if mesh.shape["dom"] <= 8 else local_hops,
        mesh=mesh, in_specs=in_specs, out_specs=out_specs, check_vma=False)
```
